32 devices in a mesh: row: 8 (over y, x, core), col: 4 (over z).
Axes of the slice: x: 2, y: 2, z: 4, core: 2. Of those that a mesh axis runs over, the one named last changes fastest.
Arguments:
- input_feat: bfloat16 [512, 8192], P('row', 'col'), may hold values from -8 to 8
- weight: bfloat16 [512, 512], replicated, may hold values from -0.25 to 0.25
- tile_values: bfloat16 [8, 4, 8, 128, 128], P('row', 'col'), as said below
- tile_slots: int32 [8, 4, 8], P('row', 'col'), may hold values from 0 to 127, as said below
- tile_count: int32 [8, 4], P('row', 'col'), may hold values from 1 to 8, as said below
- grad_output: bfloat16 [512, 8192], P('col', 'row'), may hold values from -8 to 8
Outputs:
- output_feat: bfloat16 [512, 8192], P('col', 'row')
- weight_grad: float32 [512, 512], P('row', 'col')
- grad_input: float32 [512, 8192], P('row', 'col')
The draws below stay inside these ranges and needn't reach their ends.
Inputs may be any that keep to these rules, and one draw needn't show every extreme that they name: `tile_slots`: in every grid block the 8 entries are distinct tile positions, numbered tile row times 16 plus tile column; only the first tile_count entries of a block are used. `tile_count`: some grid block has all 8 entries live. `tile_values`: entries are zero or positive; most are zero.
All inputs are finite; a program needn't handle non-finite values.
Results may differ from the reference program's by a relative error of at most 0.014.
Values may be sent and summed in bfloat16 or wider, within the bound.
A program may use at most 64 MiB of HBM per device.

```python
import jax
import jax.numpy as jnp
from jax import lax

F = 512
TILE = 128
ROW_TILES = 8
TILE_CAP = 8
ROW_BLOCKS = 8
COL_BLOCKS = 4
ROWS_DEV = 1024
NODES = 8192
COL_TILES = 16


def draw_tile_slots(key, part):
    slot_total = ROW_TILES * COL_TILES
    scores = jax.random.randint(key, (ROW_BLOCKS, COL_BLOCKS, slot_total), 0, 1 << 20) * slot_total
    scores = scores + jnp.arange(slot_total, dtype=jnp.int32)
    order = jnp.argsort(scores, axis=-1)
    return order[:, :, :TILE_CAP].astype(jnp.int32)


def draw_tile_count(key, part):
    base = jax.random.randint(jax.random.fold_in(key, 3), (ROW_BLOCKS * COL_BLOCKS,), 1, TILE_CAP + 1)
    counts = jnp.maximum(1, base * base // TILE_CAP)
    chosen = jax.random.randint(jax.random.fold_in(key, 7), (), 0, ROW_BLOCKS * COL_BLOCKS)
    counts = counts.at[chosen].set(TILE_CAP)
    return counts.reshape(ROW_BLOCKS, COL_BLOCKS).astype(jnp.int32)


def draw_tile_values(key, part):
    shape = (ROW_BLOCKS, COL_BLOCKS, TILE_CAP, TILE, TILE)
    density = 0.0625
    tiles_per_row = COL_BLOCKS * TILE_CAP / (3.0 * ROW_TILES)
    scale = 1.0 / (density * TILE * tiles_per_row)
    present = jax.random.uniform(jax.random.fold_in(key, 11), shape, jnp.float32) < density
    level = 0.5 + jax.random.uniform(jax.random.fold_in(key, 12), shape, jnp.float32)
    row_deg = jnp.exp(jax.random.uniform(jax.random.fold_in(key, 13), shape[:3] + (TILE, 1), jnp.float32, -0.35, 0.35))
    col_deg = jnp.exp(jax.random.uniform(jax.random.fold_in(key, 14), shape[:3] + (1, TILE), jnp.float32, -0.35, 0.35))
    values = jnp.where(present, level * row_deg * col_deg * scale, 0.0)
    return values.astype(jnp.bfloat16)


def channel_field(key):
    means = jax.random.uniform(jax.random.fold_in(key, 21), (F, 1), jnp.float32, 0.5, 1.5)
    signs = jnp.where(jax.random.bernoulli(jax.random.fold_in(key, 22), 0.5, (F, 1)), 1.0, -1.0)
    noise = jnp.clip(jax.random.normal(jax.random.fold_in(key, 25), (F, NODES), jnp.float32), -4.0, 4.0)
    return (signs * means + noise).astype(jnp.bfloat16)


def draw_input_feat(key, part):
    return channel_field(jax.random.fold_in(key, 31))


def draw_grad_output(key, part):
    return channel_field(jax.random.fold_in(key, 32))


def gaussian(own_key, shape, scale, bound, kind=jnp.bfloat16):
    result = scale * jax.random.normal(own_key, shape, jnp.float32)
    return jnp.clip(result, min=-bound, max=bound).astype(kind)


def setup_inputs(seed: int = 0) -> dict:
    key_of = jax.random.split(jax.random.key(seed), 7)
    input_feat = draw_input_feat(jax.random.fold_in(key_of[6], 71), 0)
    weight = gaussian(key_of[1], (F, F), F ** -0.5, 0.25)
    tile_values = draw_tile_values(jax.random.fold_in(key_of[6], 71), 0)
    tile_slots = draw_tile_slots(jax.random.fold_in(key_of[6], 71), 0)
    tile_count = draw_tile_count(jax.random.fold_in(key_of[6], 71), 0)
    grad_output = draw_grad_output(jax.random.fold_in(key_of[6], 71), 0)
    return {"input_feat": input_feat, "weight": weight, "tile_values": tile_values, "tile_slots": tile_slots, "tile_count": tile_count, "grad_output": grad_output}


def forward_block(values, slots, live_count, columns, row_tiles):
    channels = columns.shape[0]
    tile_len = values.shape[-1]
    col_tiles = columns.shape[1] // tile_len
    blocks = columns.reshape(channels, col_tiles, tile_len).astype(jnp.float32)

    def add_group(group_idx, running):
        first_tile = group_idx * 8
        tile_vals = lax.dynamic_slice_in_dim(values, first_tile, 8, 0).astype(jnp.float32)
        slot_ids = lax.dynamic_slice_in_dim(slots, first_tile, 8, 0)
        is_live = (first_tile + jnp.arange(8, dtype=jnp.int32)) < live_count
        picked = jnp.take(blocks, slot_ids % col_tiles, axis=1)
        products = jnp.einsum("ftc,trc->tfr", picked, tile_vals, precision=lax.Precision.HIGHEST)
        target = ((slot_ids // col_tiles)[:, None] == jnp.arange(row_tiles, dtype=jnp.int32)[None, :]) & is_live[:, None]
        return running + jnp.einsum("tfr,tk->fkr", products, target.astype(jnp.float32), precision=lax.Precision.HIGHEST)

    loop_count = (live_count + 7) // 8
    running = lax.fori_loop(0, loop_count, add_group, jnp.zeros((channels, row_tiles, tile_len), jnp.float32))
    return running.reshape(channels, row_tiles * tile_len)


def backward_block(values, slots, live_count, rows, col_tiles):
    channels = rows.shape[0]
    tile_len = values.shape[-1]
    row_tiles = rows.shape[1] // tile_len
    blocks = rows.reshape(channels, row_tiles, tile_len).astype(jnp.float32)

    def add_group(group_idx, running):
        first_tile = group_idx * 8
        tile_vals = lax.dynamic_slice_in_dim(values, first_tile, 8, 0).astype(jnp.float32)
        slot_ids = lax.dynamic_slice_in_dim(slots, first_tile, 8, 0)
        is_live = (first_tile + jnp.arange(8, dtype=jnp.int32)) < live_count
        picked = jnp.take(blocks, slot_ids // col_tiles, axis=1)
        products = jnp.einsum("ftr,trc->tfc", picked, tile_vals, precision=lax.Precision.HIGHEST)
        target = ((slot_ids % col_tiles)[:, None] == jnp.arange(col_tiles, dtype=jnp.int32)[None, :]) & is_live[:, None]
        return running + jnp.einsum("tfc,tk->fkc", products, target.astype(jnp.float32), precision=lax.Precision.HIGHEST)

    loop_count = (live_count + 7) // 8
    running = lax.fori_loop(0, loop_count, add_group, jnp.zeros((channels, col_tiles, tile_len), jnp.float32))
    return running.reshape(channels, col_tiles * tile_len)


def rounded_term(term):
    return lax.optimization_barrier(term.astype(jnp.bfloat16)).astype(jnp.float32)


def reference(input_feat, weight, tile_values, tile_slots, tile_count, grad_output):
    cols_block = COL_TILES * TILE

    def row_block(row_idx):
        def add_col(running, col_idx):
            columns = lax.dynamic_slice_in_dim(input_feat, col_idx * cols_block, cols_block, 1)
            term = forward_block(tile_values[row_idx, col_idx], tile_slots[row_idx, col_idx], tile_count[row_idx, col_idx], columns, ROW_TILES)
            return running + rounded_term(term), None

        start_sum = jnp.zeros((F, ROWS_DEV), jnp.float32)
        total, unused = lax.scan(add_col, start_sum, jnp.arange(COL_BLOCKS, dtype=jnp.int32))
        return total

    row_sums = lax.map(row_block, jnp.arange(ROW_BLOCKS, dtype=jnp.int32))
    aggregate = jnp.transpose(row_sums, (1, 0, 2)).reshape(F, NODES).astype(jnp.bfloat16)
    pre_act = jnp.dot(weight.T, aggregate, preferred_element_type=jnp.float32)
    sigmoid = jax.nn.sigmoid(pre_act)
    output_feat = (pre_act * sigmoid).astype(jnp.bfloat16)
    grad_pre = (grad_output.astype(jnp.float32) * sigmoid * (1.0 + pre_act * (1.0 - sigmoid))).astype(jnp.bfloat16)
    agg_blocks = aggregate.reshape(F, ROW_BLOCKS, ROWS_DEV).astype(jnp.float32)
    pre_blocks = grad_pre.reshape(F, ROW_BLOCKS, ROWS_DEV).astype(jnp.float32)
    block_wgrad = jnp.einsum("fbn,gbn->bfg", agg_blocks, pre_blocks, precision=lax.Precision.HIGHEST)
    weight_grad = jnp.sum(rounded_term(block_wgrad), axis=0) * (NODES ** -0.5)
    grad_agg = jnp.dot(weight, grad_pre, preferred_element_type=jnp.float32).astype(jnp.bfloat16)

    def col_block(col_idx):
        def add_row(running, row_idx):
            rows = lax.dynamic_slice_in_dim(grad_agg, row_idx * ROWS_DEV, ROWS_DEV, 1)
            term = backward_block(tile_values[row_idx, col_idx], tile_slots[row_idx, col_idx], tile_count[row_idx, col_idx], rows, COL_TILES)
            return running + rounded_term(term), None

        start_sum = jnp.zeros((F, cols_block), jnp.float32)
        total, unused = lax.scan(add_row, start_sum, jnp.arange(ROW_BLOCKS, dtype=jnp.int32))
        return total

    col_sums = lax.map(col_block, jnp.arange(COL_BLOCKS, dtype=jnp.int32))
    grad_input = jnp.transpose(col_sums, (1, 0, 2)).reshape(F, NODES)
    return (output_feat, weight_grad, grad_input)
```

```python
import functools

import jax
import jax.numpy as jnp
from jax import lax
from jax.experimental import pallas as pl
from jax.experimental.pallas import tpu as pltpu
from jax.sharding import PartitionSpec as P

F32, BF16 = jnp.float32, jnp.bfloat16


def fused(
    R, C, x_ref, w_ref, tv_ref, slots_ref, count_ref, go_ref, of_ref, wg_ref, gi_ref,
    tv_all, xf, pout, prx, agg_s, agg_full, go_full, of_s, of_rx, w_s, w_rx, w2_s, w2_rx,
    ga_s, ga_rx, ga_all,
    sdir, sfwd, rtv, sgo, rgo, szr, rzr, sa, ra, sof, rof, swz, rwz, swr, rwr, sg, rg, sgz, rgz,
):
    T, L = tv_ref.shape[2], tv_ref.shape[3]
    FR, NB = x_ref.shape
    FC, NR = go_ref.shape
    F = w_ref.shape[0]
    RT, CT, SH = NR // L, NB // L, NR // C
    per = SH // L
    mi, mj = lax.axis_index("row"), lax.axis_index("col")
    sib = mi + 1 - 2 * lax.rem(mi, 2)
    half = R // 2

    def rowp(p):
        return {"row": p}

    def colp(p):
        return {"col": p}

    def rcopy(src, dst, ss, rs, dev):
        return pltpu.make_async_remote_copy(
            src_ref=src, dst_ref=dst, send_sem=ss, recv_sem=rs, device_id=dev,
            device_id_type=pl.DeviceIdType.MESH,
        )

    def rows(d):
        return lax.rem(mi + d, R)

    def cols(d):
        return lax.rem(mj + d, C)

    barrier = pltpu.get_barrier_semaphore()
    for d in range(1, R):
        pl.semaphore_signal(barrier, inc=1, device_id=rowp(rows(d)), device_id_type=pl.DeviceIdType.MESH)
    for d in range(1, C):
        pl.semaphore_signal(barrier, inc=1, device_id=colp(cols(d)), device_id_type=pl.DeviceIdType.MESH)

    tv_all[mi, 0 : T * L, :] = tv_ref[0, 0].reshape(T * L, L)
    count = count_ref[0, 0]
    lines = []
    for t in range(T):
        lines.append(jnp.full((1, L), lax.rem(slots_ref[0, 0, t], CT), jnp.int32))
    for t in range(T):
        home = jnp.where(t < count, lax.div(slots_ref[0, 0, t], CT), RT)
        lines.append(jnp.full((1, L), home, jnp.int32))
    tv_all[mi, T * L : T * L + 2 * T, :] = jnp.concatenate(lines, axis=0).astype(F32).astype(BF16)
    xf[...] = x_ref[...].astype(F32)

    pl.semaphore_wait(barrier, R + C - 2)

    for m in range(1, half):
        rcopy(tv_all.at[mi], tv_all.at[mi], sdir.at[m], rtv.at[mi], rowp(rows(2 * m))).start()
    for d in range(1, C):
        rcopy(
            go_ref.at[:, pl.ds(pl.multiple_of(cols(d) * SH, SH), SH)],
            go_full.at[mj], sgo.at[d], rgo.at[mj], colp(cols(d)),
        ).start()
    go_full[mj] = go_ref[:, pl.ds(pl.multiple_of(mj * SH, SH), SH)]

    def forward(b):
        info = tv_all[b, T * L : T * L + 2 * T, :].astype(F32)
        prods = []
        for t in range(T):
            colv = jnp.broadcast_to(info[t : t + 1, :], (FR, L))
            pick = jnp.zeros((FR, L), F32)
            for c in range(CT):
                pick = jnp.where(colv == c, xf[:, c * L : (c + 1) * L], pick)
            prods.append(
                lax.dot_general(
                    pick.astype(BF16), tv_all[b, t * L : (t + 1) * L, :],
                    (((1,), (1,)), ((), ())), preferred_element_type=F32,
                )
            )
        for k in range(RT):
            acc = jnp.zeros((FR, L), F32)
            for t in range(T):
                rowv = jnp.broadcast_to(info[T + t : T + t + 1, :], (FR, L))
                acc = acc + jnp.where(rowv == k, prods[t], 0.0)
            pout[k // per, b, :, (k % per) * L : (k % per + 1) * L] = acc.astype(BF16)
        for d in range(1, C):
            rcopy(
                pout.at[cols(d), b], prx.at[mj, b], szr.at[b, d], rzr.at[b, mj], colp(cols(d))
            ).start()

    def wait_tv(b):
        rcopy(tv_all.at[b], tv_all.at[b], sfwd.at[0], rtv.at[b], rowp(sib)).wait_recv()

    def gather_step(m, carry):
        p, q = rows(2 * m), lax.rem(sib + 2 * m, R)

        @pl.when(m > 0)
        def _():
            wait_tv(p)

        rcopy(tv_all.at[p], tv_all.at[p], sfwd.at[m], rtv.at[p], rowp(sib)).start()

        def one(h, carry):
            b = jnp.where(h == 0, p, q)

            @pl.when(h == 1)
            def _():
                wait_tv(q)

            forward(b)
            return carry

        return lax.fori_loop(0, 2, one, carry)

    lax.fori_loop(0, half, gather_step, 0)

    def reduce_step(n, carry):
        m, h = lax.div(n, 2), lax.rem(n, 2)
        b = lax.rem(jnp.where(h == 0, mi, sib) + 2 * m, R)
        total = pout[mj, b].astype(F32)
        for d in range(1, C):
            rcopy(pout.at[cols(d), b], prx.at[cols(d), b], szr.at[b, d], rzr.at[b, cols(d)], colp(cols(d))).wait_recv()
            total = total + prx[cols(d), b].astype(F32)
        agg_s[b] = total.astype(BF16)

        @pl.when(b == mi)
        def _():
            agg_full[mi] = agg_s[mi]

        @pl.when(b != mi)
        def _():
            rcopy(agg_s.at[b], agg_full.at[mi], sa.at[b], ra.at[mi], rowp(b)).start()

        return carry

    lax.fori_loop(0, R, reduce_step, 0)

    for d in range(1, C):
        rcopy(go_full.at[cols(d)], go_full.at[cols(d)], sgo.at[d], rgo.at[cols(d)], colp(cols(d))).wait_recv()
    for d in range(1, R):
        p = rows(d)
        rcopy(agg_s.at[p], agg_full.at[p], sa.at[p], ra.at[p], rowp(p)).wait_recv()

    agg = agg_full[...].reshape(F, SH)
    pre = lax.dot_general(w_ref[...], agg, (((0,), (0,)), ((), ())), preferred_element_type=F32)
    s = 1.0 / (1.0 + jnp.exp(-pre))
    gp = (go_full[...].reshape(F, SH).astype(F32) * s * (1.0 + pre * (1.0 - s))).astype(BF16)
    ga_s[...] = jnp.dot(w_ref[...], gp, preferred_element_type=F32).astype(BF16).reshape(R, FR, SH)
    for d in range(1, R):
        p = rows(d)
        rcopy(ga_s.at[p], ga_rx.at[mi], sg.at[p], rg.at[mi], rowp(p)).start()
    of_s[...] = (pre * s).astype(BF16).reshape(C, FC, SH)
    ga_rx[mi] = ga_s[mi]

    def spread(n, carry):
        p = rows(n)

        @pl.when(n > 0)
        def _():
            rcopy(ga_s.at[p], ga_rx.at[p], sg.at[p], rg.at[p], rowp(p)).wait_recv()

        for d in range(1, C):
            rcopy(ga_rx.at[p], ga_all.at[mj, p], sgz.at[p, d], rgz.at[p, mj], colp(cols(d))).start()
        ga_all[mj, p] = ga_rx[p]
        return carry

    lax.fori_loop(0, R, spread, 0)

    for j in range(C):
        w_s[j] = lax.dot_general(
            agg, gp[j * FC : (j + 1) * FC, :], (((1,), (1,)), ((), ())), preferred_element_type=F32
        ).astype(BF16)
    for d in range(1, C):
        q = cols(d)
        rcopy(w_s.at[q], w_rx.at[mj], swz.at[d], rwz.at[mj], colp(q)).start()
        rcopy(of_s.at[q], of_rx.at[mj], sof.at[d], rof.at[mj], colp(q)).start()
    of_rx[mj] = of_s[mj]

    gi_ref[...] = jnp.zeros_like(gi_ref)

    def backward(n, carry):
        b = rows(n)
        for d in range(1, C):
            q = cols(d)
            rcopy(ga_rx.at[b], ga_all.at[q, b], sgz.at[b, d], rgz.at[b, q], colp(q)).wait_recv()
        info = tv_all[b, T * L : T * L + 2 * T, :].astype(F32)
        prods = []
        for t in range(T):
            rowv = jnp.broadcast_to(info[T + t : T + t + 1, :], (FR, L))
            pick = jnp.zeros((FR, L), F32)
            for k in range(RT):
                part = ga_all[k // per, b, :, (k % per) * L : (k % per + 1) * L].astype(F32)
                pick = jnp.where(rowv == k, part, pick)
            prods.append(
                jnp.dot(pick.astype(BF16), tv_all[b, t * L : (t + 1) * L, :], preferred_element_type=F32)
            )
        for c in range(CT):
            acc = gi_ref[:, c * L : (c + 1) * L]
            for t in range(T):
                colv = jnp.broadcast_to(info[t : t + 1, :], (FR, L))
                acc = acc + jnp.where(colv == c, prods[t], 0.0)
            gi_ref[:, c * L : (c + 1) * L] = acc
        return carry

    lax.fori_loop(0, R, backward, 0)

    total = w_s[mj].astype(F32)
    for d in range(1, C):
        q = cols(d)
        rcopy(w_s.at[q], w_rx.at[q], swz.at[d], rwz.at[q], colp(q)).wait_recv()
        total = total + w_rx[q].astype(F32)
    w2_s[...] = total.astype(BF16).reshape(R, FR, FC)
    for d in range(1, R):
        p = rows(d)
        rcopy(w2_s.at[p], w2_rx.at[mi], swr.at[p], rwr.at[mi], rowp(p)).start()
    for d in range(1, C):
        q = cols(d)
        rcopy(of_s.at[q], of_rx.at[q], sof.at[d], rof.at[q], colp(q)).wait_recv()
    for j in range(C):
        of_ref[:, j * SH : (j + 1) * SH] = of_rx[j]
    total = w2_s[mi].astype(F32)
    for d in range(1, R):
        p = rows(d)
        rcopy(w2_s.at[p], w2_rx.at[p], swr.at[p], rwr.at[p], rowp(p)).wait_recv()
        total = total + w2_rx[p].astype(F32)
    wg_ref[...] = total * (NR * R) ** -0.5

    for m in range(1, half):
        rcopy(tv_all.at[mi], tv_all.at[mi], sdir.at[m], rtv.at[mi], rowp(rows(2 * m))).wait_send()
    for m in range(half):
        rcopy(tv_all.at[mi], tv_all.at[mi], sfwd.at[m], rtv.at[mi], rowp(sib)).wait_send()
    for d in range(1, C):
        q = cols(d)
        rcopy(go_full.at[mj], go_full.at[mj], sgo.at[d], rgo.at[mj], colp(q)).wait_send()
        rcopy(w_s.at[q], w_rx.at[mj], swz.at[d], rwz.at[mj], colp(q)).wait_send()
        rcopy(of_s.at[q], of_rx.at[mj], sof.at[d], rof.at[mj], colp(q)).wait_send()

    def drain(n, carry):
        p = rows(n)
        for d in range(1, C):
            q = cols(d)
            rcopy(pout.at[q, p], prx.at[mj, p], szr.at[p, d], rzr.at[p, mj], colp(q)).wait_send()
            rcopy(ga_rx.at[p], ga_all.at[mj, p], sgz.at[p, d], rgz.at[p, mj], colp(q)).wait_send()

        @pl.when(n > 0)
        def _():
            rcopy(agg_s.at[p], agg_full.at[mi], sa.at[p], ra.at[mi], rowp(p)).wait_send()
            rcopy(ga_s.at[p], ga_rx.at[mi], sg.at[p], rg.at[mi], rowp(p)).wait_send()
            rcopy(w2_s.at[p], w2_rx.at[mi], swr.at[p], rwr.at[mi], rowp(p)).wait_send()

        return carry

    lax.fori_loop(0, R, drain, 0)


def fused_device(R, C, x, w, tv, slots, count, go):
    T, L = tv.shape[2], tv.shape[3]
    FR, NB = x.shape
    FC, NR = go.shape
    F, SH = w.shape[0], NR // C
    vm, dma = pltpu.VMEM, pltpu.SemaphoreType.DMA
    scratch = [
        vm((R, T * L + 2 * T, L), BF16), vm((FR, NB), F32),
        vm((C, R, FR, SH), BF16), vm((C, R, FR, SH), BF16),
        vm((R, FR, SH), BF16), vm((R, FR, SH), BF16), vm((C, FC, SH), BF16),
        vm((C, FC, SH), BF16), vm((C, FC, SH), BF16),
        vm((C, F, FC), BF16), vm((C, F, FC), BF16),
        vm((R, FR, FC), BF16), vm((R, FR, FC), BF16),
        vm((R, FR, SH), BF16), vm((R, FR, SH), BF16), vm((C, R, FR, SH), BF16),
        dma((R // 2,)), dma((R // 2,)), dma((R,)), dma((C,)), dma((C,)),
        dma((R, C)), dma((R, C)), dma((R,)), dma((R,)), dma((C,)), dma((C,)),
        dma((C,)), dma((C,)), dma((R,)), dma((R,)), dma((R,)), dma((R,)), dma((R, C)), dma((R, C)),
    ]
    vmem, smem = pl.BlockSpec(memory_space=pltpu.VMEM), pl.BlockSpec(memory_space=pltpu.SMEM)
    return pl.pallas_call(
        functools.partial(fused, R, C),
        out_shape=(
            jax.ShapeDtypeStruct((FC, NR), BF16),
            jax.ShapeDtypeStruct((FR, FC), F32),
            jax.ShapeDtypeStruct((FR, NB), F32),
        ),
        in_specs=[vmem, vmem, vmem, smem, smem, vmem],
        out_specs=(vmem, vmem, vmem),
        scratch_shapes=scratch,
        compiler_params=pltpu.CompilerParams(
            collective_id=0, has_side_effects=True, vmem_limit_bytes=40 * 1024 * 1024
        ),
    )(x, w, tv, slots, count, go)


def gather(x, axis):
    n = lax.axis_size(axis)
    spread = jnp.broadcast_to(x[None], (n,) + x.shape)
    return lax.all_to_all(spread, axis, 0, 0).reshape((n * x.shape[0],) + x.shape[1:])


def scatter_sum(x, axis):
    n = lax.axis_size(axis)
    parts = lax.all_to_all(x.reshape((n, x.shape[0] // n) + x.shape[1:]), axis, 0, 0)
    return jnp.sum(parts.astype(F32), axis=0)


def forward_block(values, slots, live_count, columns, row_tiles, loop_count):
    channels = columns.shape[0]
    tile_len = values.shape[-1]
    col_tiles = columns.shape[1] // tile_len
    blocks = columns.reshape(channels, col_tiles, tile_len)

    def forward_add_group(group_idx, running):
        first_tile = group_idx * 8
        is_live = first_tile + jnp.arange(8, dtype=jnp.int32) < live_count
        picked = jnp.take(blocks, slots % col_tiles, axis=1)
        products = jnp.einsum("ftc,trc->tfr", picked, values, preferred_element_type=jnp.float32)
        target = (
            (slots // col_tiles)[:, None] == jnp.arange(row_tiles, dtype=jnp.int32)[None, :]
        ) & is_live[:, None]
        return running + jnp.einsum(
            "tfr,tk->fkr", products, target.astype(jnp.float32), precision=lax.Precision.HIGHEST
        )

    running = lax.fori_loop(
        0, loop_count, forward_add_group, jnp.zeros((channels, row_tiles, tile_len), jnp.float32)
    )
    return running.reshape(channels, row_tiles * tile_len)


def backward_block(values, slots, live_count, rows, col_tiles, loop_count):
    channels = rows.shape[0]
    tile_len = values.shape[-1]
    row_tiles = rows.shape[1] // tile_len
    blocks = rows.reshape(channels, row_tiles, tile_len)

    def backward_add_group(group_idx, running):
        first_tile = group_idx * 8
        is_live = first_tile + jnp.arange(8, dtype=jnp.int32) < live_count
        picked = jnp.take(blocks, slots // col_tiles, axis=1)
        products = jnp.einsum("ftr,trc->tfc", picked, values, preferred_element_type=jnp.float32)
        target = (
            (slots % col_tiles)[:, None] == jnp.arange(col_tiles, dtype=jnp.int32)[None, :]
        ) & is_live[:, None]
        return running + jnp.einsum(
            "tfc,tk->fkc", products, target.astype(jnp.float32), precision=lax.Precision.HIGHEST
        )

    running = lax.fori_loop(
        0, loop_count, backward_add_group, jnp.zeros((channels, col_tiles, tile_len), jnp.float32)
    )
    return running.reshape(channels, col_tiles * tile_len)


def per_device(input_feat, weight, tile_values, tile_slots, tile_count, grad_output):
    values = tile_values[0, 0]
    slots = tile_slots[0, 0]
    live_count = tile_count[0, 0]
    tile_len = values.shape[-1]
    row_tiles = grad_output.shape[1] // tile_len
    col_tiles = input_feat.shape[1] // tile_len
    loop_count = values.shape[0] // 8
    partial_agg = forward_block(
        values,
        slots,
        live_count,
        gather(input_feat, "row"),
        row_tiles,
        loop_count,
    )
    aggregate = gather(scatter_sum(partial_agg.astype(jnp.bfloat16), "col").astype(jnp.bfloat16), "col")
    out_width = weight.shape[1] // lax.axis_size("col")
    weight_cols = lax.dynamic_slice_in_dim(weight, lax.axis_index("col") * out_width, out_width, 1)
    pre_act = lax.dot_general(
        weight_cols, aggregate, (((0,), (0,)), ((), ())), preferred_element_type=jnp.float32
    )
    sigmoid = jax.nn.sigmoid(pre_act)
    output_feat = (pre_act * sigmoid).astype(jnp.bfloat16)
    grad_pre = (
        grad_output.astype(jnp.float32) * sigmoid * (1.0 + pre_act * (1.0 - sigmoid))
    ).astype(jnp.bfloat16)
    weight_part = lax.dot_general(
        aggregate, grad_pre, (((1,), (1,)), ((), ())), preferred_element_type=jnp.float32
    )
    grad_full = gather(grad_pre, "col")
    grad_agg = jnp.dot(weight, grad_full, preferred_element_type=jnp.float32).astype(jnp.bfloat16)
    input_part = backward_block(values, slots, live_count, grad_agg, col_tiles, loop_count)
    grad_input = scatter_sum(input_part.astype(jnp.bfloat16), "row")
    weight_share = scatter_sum(weight_part.astype(jnp.bfloat16), "row")
    node_total = grad_output.shape[1] * lax.axis_size("row")
    return (output_feat, weight_share * node_total ** (-0.5), grad_input)


def solution(mesh):
    in_specs = (
        P("row", "col"),
        P(),
        P("row", "col", None, None, None),
        P("row", "col", None),
        P("row", "col"),
        P("col", "row"),
    )
    out_specs = (P("col", "row"), P("row", "col"), P("row", "col"))
    R, C = mesh.shape["row"], mesh.shape["col"]

    def device(x, w, tv, slots, count, go):
        if R % 2 == 0 and go.shape[1] % (C * tv.shape[-1]) == 0 and x.shape[0] % 16 == 0:
            return fused_device(R, C, x, w, tv, slots, count, go)
        return per_device(x, w, tv, slots, count, go)

    return jax.shard_map(
        device, mesh=mesh, in_specs=in_specs, out_specs=out_specs, check_vma=False
    )
```

```python
import functools

import jax
import jax.numpy as jnp
from jax import lax
from jax.experimental import pallas as pl
from jax.experimental.pallas import tpu as pltpu
from jax.sharding import PartitionSpec as P

F32, BF16 = jnp.float32, jnp.bfloat16


def fused(
    R, C, T, x_hbm, w_hbm, tv_hbm, slots_ref, count_ref, go_hbm, of_ref, wg_ref, gi_ref,
    x_ref, w_ref, go_ref, lsem,
    tv_all, xf, pout, prx, agg_s, agg_full, go_full, of_s, of_rx, w_s, w_rx, w2_s, w2_rx,
    ga_s, ga_rx, ga_all,
    sdir, sfwd, rtv, sgo, rgo, szr, rzr, sa, ra, sof, rof, swz, rwz, swr, rwr, sg, rg, sgz, rgz,
):
    L = tv_hbm.shape[1]
    FR, NB = x_ref.shape
    FC, NR = go_ref.shape
    F = w_ref.shape[0]
    RT, CT, SH = NR // L, NB // L, NR // C
    per = SH // L
    mi, mj = lax.axis_index("row"), lax.axis_index("col")
    sib = mi + 1 - 2 * lax.rem(mi, 2)
    half = R // 2

    def rowp(p):
        return {"row": p}

    def colp(p):
        return {"col": p}

    def rcopy(src, dst, ss, rs, dev):
        return pltpu.make_async_remote_copy(
            src_ref=src, dst_ref=dst, send_sem=ss, recv_sem=rs, device_id=dev,
            device_id_type=pl.DeviceIdType.MESH,
        )

    def rows(d):
        return lax.rem(mi + d, R)

    def cols(d):
        return lax.rem(mj + d, C)

    loads = [
        pltpu.make_async_copy(tv_hbm, tv_all.at[mi, 0 : T * L], lsem.at[0]),
        pltpu.make_async_copy(go_hbm, go_ref, lsem.at[1]),
        pltpu.make_async_copy(x_hbm, x_ref, lsem.at[2]),
        pltpu.make_async_copy(w_hbm, w_ref, lsem.at[3]),
    ]
    for load in loads:
        load.start()

    barrier = pltpu.get_barrier_semaphore()
    for d in range(1, R):
        pl.semaphore_signal(barrier, inc=1, device_id=rowp(rows(d)), device_id_type=pl.DeviceIdType.MESH)
    for d in range(1, C):
        pl.semaphore_signal(barrier, inc=1, device_id=colp(cols(d)), device_id_type=pl.DeviceIdType.MESH)

    count = count_ref[0, 0]
    lines = []
    for t in range(T):
        lines.append(jnp.full((1, L), lax.rem(slots_ref[0, 0, t], CT), jnp.int32))
    for t in range(T):
        home = jnp.where(t < count, lax.div(slots_ref[0, 0, t], CT), RT)
        lines.append(jnp.full((1, L), home, jnp.int32))
    tv_all[mi, T * L : T * L + 2 * T, :] = jnp.concatenate(lines, axis=0).astype(F32).astype(BF16)
    pl.semaphore_wait(barrier, R + C - 2)
    loads[0].wait()
    loads[1].wait()

    for m in range(1, half):
        rcopy(tv_all.at[mi], tv_all.at[mi], sdir.at[m], rtv.at[mi], rowp(rows(2 * m))).start()
    for d in range(1, C):
        rcopy(
            go_ref.at[:, pl.ds(pl.multiple_of(cols(d) * SH, SH), SH)],
            go_full.at[mj], sgo.at[d], rgo.at[mj], colp(cols(d)),
        ).start()
    go_full[mj] = go_ref[:, pl.ds(pl.multiple_of(mj * SH, SH), SH)]

    loads[2].wait()
    xf[...] = x_ref[...].astype(F32)

    def forward(b):
        info = tv_all[b, T * L : T * L + 2 * T, :].astype(F32)
        prods = []
        for t in range(T):
            colv = jnp.broadcast_to(info[t : t + 1, :], (FR, L))
            pick = jnp.zeros((FR, L), F32)
            for c in range(CT):
                pick = jnp.where(colv == c, xf[:, c * L : (c + 1) * L], pick)
            prods.append(
                lax.dot_general(
                    pick.astype(BF16), tv_all[b, t * L : (t + 1) * L, :],
                    (((1,), (1,)), ((), ())), preferred_element_type=F32,
                )
            )
        for k in range(RT):
            acc = jnp.zeros((FR, L), F32)
            for t in range(T):
                rowv = jnp.broadcast_to(info[T + t : T + t + 1, :], (FR, L))
                acc = acc + jnp.where(rowv == k, prods[t], 0.0)
            pout[k // per, b, :, (k % per) * L : (k % per + 1) * L] = acc.astype(BF16)
        for d in range(1, C):
            rcopy(
                pout.at[cols(d), b], prx.at[mj, b], szr.at[b, d], rzr.at[b, mj], colp(cols(d))
            ).start()

    def wait_tv(b):
        rcopy(tv_all.at[b], tv_all.at[b], sfwd.at[0], rtv.at[b], rowp(sib)).wait_recv()

    def gather_step(m, carry):
        p, q = rows(2 * m), lax.rem(sib + 2 * m, R)

        @pl.when(m > 0)
        def _():
            wait_tv(p)

        rcopy(tv_all.at[p], tv_all.at[p], sfwd.at[m], rtv.at[p], rowp(sib)).start()

        def one(h, carry):
            b = jnp.where(h == 0, p, q)

            @pl.when(h == 1)
            def _():
                wait_tv(q)

            forward(b)
            return carry

        return lax.fori_loop(0, 2, one, carry)

    lax.fori_loop(0, half, gather_step, 0)

    def reduce_step(n, carry):
        m, h = lax.div(n, 2), lax.rem(n, 2)
        b = lax.rem(jnp.where(h == 0, mi, sib) + 2 * m, R)
        total = pout[mj, b].astype(F32)
        for d in range(1, C):
            rcopy(pout.at[cols(d), b], prx.at[cols(d), b], szr.at[b, d], rzr.at[b, cols(d)], colp(cols(d))).wait_recv()
            total = total + prx[cols(d), b].astype(F32)
        agg_s[b] = total.astype(BF16)

        @pl.when(b == mi)
        def _():
            agg_full[mi] = agg_s[mi]

        @pl.when(b != mi)
        def _():
            rcopy(agg_s.at[b], agg_full.at[mi], sa.at[b], ra.at[mi], rowp(b)).start()

        return carry

    lax.fori_loop(0, R, reduce_step, 0)

    for d in range(1, C):
        rcopy(go_full.at[cols(d)], go_full.at[cols(d)], sgo.at[d], rgo.at[cols(d)], colp(cols(d))).wait_recv()
    for d in range(1, R):
        p = rows(d)
        rcopy(agg_s.at[p], agg_full.at[p], sa.at[p], ra.at[p], rowp(p)).wait_recv()

    loads[3].wait()
    agg = agg_full[...].reshape(F, SH)
    pre = lax.dot_general(w_ref[...], agg, (((0,), (0,)), ((), ())), preferred_element_type=F32)
    s = 1.0 / (1.0 + jnp.exp(-pre))
    gp = (go_full[...].reshape(F, SH).astype(F32) * s * (1.0 + pre * (1.0 - s))).astype(BF16)
    ga_s[...] = jnp.dot(w_ref[...], gp, preferred_element_type=F32).astype(BF16).reshape(R, FR, SH)
    for d in range(1, R):
        p = rows(d)
        rcopy(ga_s.at[p], ga_rx.at[mi], sg.at[p], rg.at[mi], rowp(p)).start()
    of_s[...] = (pre * s).astype(BF16).reshape(C, FC, SH)
    ga_rx[mi] = ga_s[mi]

    def spread(n, carry):
        p = rows(n)

        @pl.when(n > 0)
        def _():
            rcopy(ga_s.at[p], ga_rx.at[p], sg.at[p], rg.at[p], rowp(p)).wait_recv()

        for d in range(1, C):
            rcopy(ga_rx.at[p], ga_all.at[mj, p], sgz.at[p, d], rgz.at[p, mj], colp(cols(d))).start()
        ga_all[mj, p] = ga_rx[p]
        return carry

    lax.fori_loop(0, R, spread, 0)

    w_s[...] = lax.dot_general(
        agg, gp, (((1,), (1,)), ((), ())), preferred_element_type=F32
    ).astype(BF16).reshape(R, FR, F)
    for d in range(1, R):
        p = rows(d)
        rcopy(w_s.at[p], w_rx.at[mi], swr.at[p], rwr.at[mi], rowp(p)).start()
    for d in range(1, C):
        q = cols(d)
        rcopy(of_s.at[q], of_rx.at[mj], sof.at[d], rof.at[mj], colp(q)).start()
    of_rx[mj] = of_s[mj]

    total = w_s[mi].astype(F32)
    for d in range(1, R):
        p = rows(d)
        rcopy(w_s.at[p], w_rx.at[p], swr.at[p], rwr.at[p], rowp(p)).wait_recv()
        total = total + w_rx[p].astype(F32)
    for j in range(C):
        w2_s[j] = total[:, j * FC : (j + 1) * FC].astype(BF16)
    for d in range(1, C):
        q = cols(d)
        rcopy(w2_s.at[q], w2_rx.at[mj], swz.at[d], rwz.at[mj], colp(q)).start()

    gi_ref[...] = jnp.zeros_like(gi_ref)

    def backward(n, carry):
        b = rows(n)
        for d in range(1, C):
            q = cols(d)
            rcopy(ga_rx.at[b], ga_all.at[q, b], sgz.at[b, d], rgz.at[b, q], colp(q)).wait_recv()
        info = tv_all[b, T * L : T * L + 2 * T, :].astype(F32)
        prods = []
        for t in range(T):
            rowv = jnp.broadcast_to(info[T + t : T + t + 1, :], (FR, L))
            pick = jnp.zeros((FR, L), F32)
            for k in range(RT):
                part = ga_all[k // per, b, :, (k % per) * L : (k % per + 1) * L].astype(F32)
                pick = jnp.where(rowv == k, part, pick)
            prods.append(
                jnp.dot(pick.astype(BF16), tv_all[b, t * L : (t + 1) * L, :], preferred_element_type=F32)
            )
        for c in range(CT):
            acc = gi_ref[:, c * L : (c + 1) * L]
            for t in range(T):
                colv = jnp.broadcast_to(info[t : t + 1, :], (FR, L))
                acc = acc + jnp.where(colv == c, prods[t], 0.0)
            gi_ref[:, c * L : (c + 1) * L] = acc
        return carry

    lax.fori_loop(0, R, backward, 0)

    for d in range(1, C):
        q = cols(d)
        rcopy(of_s.at[q], of_rx.at[q], sof.at[d], rof.at[q], colp(q)).wait_recv()
    for j in range(C):
        of_ref[:, j * SH : (j + 1) * SH] = of_rx[j]
    total = w2_s[mj].astype(F32)
    for d in range(1, C):
        q = cols(d)
        rcopy(w2_s.at[q], w2_rx.at[q], swz.at[d], rwz.at[q], colp(q)).wait_recv()
        total = total + w2_rx[q].astype(F32)
    wg_ref[...] = total * (NR * R) ** -0.5

    for m in range(1, half):
        rcopy(tv_all.at[mi], tv_all.at[mi], sdir.at[m], rtv.at[mi], rowp(rows(2 * m))).wait_send()
    for m in range(half):
        rcopy(tv_all.at[mi], tv_all.at[mi], sfwd.at[m], rtv.at[mi], rowp(sib)).wait_send()
    for d in range(1, C):
        q = cols(d)
        rcopy(go_full.at[mj], go_full.at[mj], sgo.at[d], rgo.at[mj], colp(q)).wait_send()
        rcopy(w2_s.at[q], w2_rx.at[mj], swz.at[d], rwz.at[mj], colp(q)).wait_send()
        rcopy(of_s.at[q], of_rx.at[mj], sof.at[d], rof.at[mj], colp(q)).wait_send()

    def drain(n, carry):
        p = rows(n)
        for d in range(1, C):
            q = cols(d)
            rcopy(pout.at[q, p], prx.at[mj, p], szr.at[p, d], rzr.at[p, mj], colp(q)).wait_send()
            rcopy(ga_rx.at[p], ga_all.at[mj, p], sgz.at[p, d], rgz.at[p, mj], colp(q)).wait_send()

        @pl.when(n > 0)
        def _():
            rcopy(agg_s.at[p], agg_full.at[mi], sa.at[p], ra.at[mi], rowp(p)).wait_send()
            rcopy(ga_s.at[p], ga_rx.at[mi], sg.at[p], rg.at[mi], rowp(p)).wait_send()
            rcopy(w_s.at[p], w_rx.at[mi], swr.at[p], rwr.at[mi], rowp(p)).wait_send()

        return carry

    lax.fori_loop(0, R, drain, 0)


def fused_device(R, C, x, w, tv, slots, count, go):
    T, L = tv.shape[2], tv.shape[3]
    FR, NB = x.shape
    FC, NR = go.shape
    F, SH = w.shape[0], NR // C
    vm, dma = pltpu.VMEM, pltpu.SemaphoreType.DMA
    scratch = [
        vm((FR, NB), BF16), vm((F, F), BF16), vm((FC, NR), BF16), dma((4,)),
        vm((R, T * L + 2 * T, L), BF16), vm((FR, NB), F32),
        vm((C, R, FR, SH), BF16), vm((C, R, FR, SH), BF16),
        vm((R, FR, SH), BF16), vm((R, FR, SH), BF16), vm((C, FC, SH), BF16),
        vm((C, FC, SH), BF16), vm((C, FC, SH), BF16),
        vm((R, FR, F), BF16), vm((R, FR, F), BF16),
        vm((C, FR, FC), BF16), vm((C, FR, FC), BF16),
        vm((R, FR, SH), BF16), vm((R, FR, SH), BF16), vm((C, R, FR, SH), BF16),
        dma((R // 2,)), dma((R // 2,)), dma((R,)), dma((C,)), dma((C,)),
        dma((R, C)), dma((R, C)), dma((R,)), dma((R,)), dma((C,)), dma((C,)),
        dma((C,)), dma((C,)), dma((R,)), dma((R,)), dma((R,)), dma((R,)), dma((R, C)), dma((R, C)),
    ]
    vmem, smem = pl.BlockSpec(memory_space=pltpu.VMEM), pl.BlockSpec(memory_space=pltpu.SMEM)
    hbm = pl.BlockSpec(memory_space=pltpu.HBM)
    return pl.pallas_call(
        functools.partial(fused, R, C, T),
        out_shape=(
            jax.ShapeDtypeStruct((FC, NR), BF16),
            jax.ShapeDtypeStruct((FR, FC), F32),
            jax.ShapeDtypeStruct((FR, NB), F32),
        ),
        in_specs=[hbm, hbm, hbm, smem, smem, hbm],
        out_specs=(vmem, vmem, vmem),
        scratch_shapes=scratch,
        compiler_params=pltpu.CompilerParams(
            collective_id=0, has_side_effects=True, vmem_limit_bytes=60 * 1024 * 1024
        ),
    )(x, w, tv.reshape(T * L, L), slots, count, go)


def gather(x, axis):
    n = lax.axis_size(axis)
    spread = jnp.broadcast_to(x[None], (n,) + x.shape)
    return lax.all_to_all(spread, axis, 0, 0).reshape((n * x.shape[0],) + x.shape[1:])


def scatter_sum(x, axis):
    n = lax.axis_size(axis)
    parts = lax.all_to_all(x.reshape((n, x.shape[0] // n) + x.shape[1:]), axis, 0, 0)
    return jnp.sum(parts.astype(F32), axis=0)


def pick_blocks(blocks, index):
    chosen = index[:, None] == jnp.arange(blocks.shape[1], dtype=jnp.int32)[None, :]
    return jnp.einsum("fkc,tk->ftc", blocks, chosen.astype(blocks.dtype))


def forward_block(values, slots, live_count, columns, row_tiles, loop_count):
    channels = columns.shape[0]
    tile_len = values.shape[-1]
    col_tiles = columns.shape[1] // tile_len
    blocks = columns.reshape(channels, col_tiles, tile_len)

    def forward_add_group(group_idx, running):
        first_tile = group_idx * 8
        is_live = first_tile + jnp.arange(8, dtype=jnp.int32) < live_count
        picked = pick_blocks(blocks, slots % col_tiles)
        products = jnp.einsum("ftc,trc->tfr", picked, values, preferred_element_type=jnp.float32)
        target = (
            (slots // col_tiles)[:, None] == jnp.arange(row_tiles, dtype=jnp.int32)[None, :]
        ) & is_live[:, None]
        return running + jnp.einsum(
            "tfr,tk->fkr", products, target.astype(jnp.float32), precision=lax.Precision.HIGHEST
        )

    running = lax.fori_loop(
        0, loop_count, forward_add_group, jnp.zeros((channels, row_tiles, tile_len), jnp.float32)
    )
    return running.reshape(channels, row_tiles * tile_len)


def backward_block(values, slots, live_count, rows, col_tiles, loop_count):
    channels = rows.shape[0]
    tile_len = values.shape[-1]
    row_tiles = rows.shape[1] // tile_len
    blocks = rows.reshape(channels, row_tiles, tile_len)

    def backward_add_group(group_idx, running):
        first_tile = group_idx * 8
        is_live = first_tile + jnp.arange(8, dtype=jnp.int32) < live_count
        picked = pick_blocks(blocks, slots // col_tiles)
        products = jnp.einsum("ftr,trc->tfc", picked, values, preferred_element_type=jnp.float32)
        target = (
            (slots % col_tiles)[:, None] == jnp.arange(col_tiles, dtype=jnp.int32)[None, :]
        ) & is_live[:, None]
        return running + jnp.einsum(
            "tfc,tk->fkc", products, target.astype(jnp.float32), precision=lax.Precision.HIGHEST
        )

    running = lax.fori_loop(
        0, loop_count, backward_add_group, jnp.zeros((channels, col_tiles, tile_len), jnp.float32)
    )
    return running.reshape(channels, col_tiles * tile_len)


def per_device(input_feat, weight, tile_values, tile_slots, tile_count, grad_output):
    values = tile_values[0, 0]
    slots = tile_slots[0, 0]
    live_count = tile_count[0, 0]
    tile_len = values.shape[-1]
    row_tiles = grad_output.shape[1] // tile_len
    col_tiles = input_feat.shape[1] // tile_len
    loop_count = values.shape[0] // 8
    partial_agg = forward_block(
        values,
        slots,
        live_count,
        gather(input_feat, "row"),
        row_tiles,
        loop_count,
    )
    aggregate = gather(scatter_sum(partial_agg.astype(jnp.bfloat16), "col").astype(jnp.bfloat16), "col")
    out_width = weight.shape[1] // lax.axis_size("col")
    weight_cols = lax.dynamic_slice_in_dim(weight, lax.axis_index("col") * out_width, out_width, 1)
    pre_act = lax.dot_general(
        weight_cols, aggregate, (((0,), (0,)), ((), ())), preferred_element_type=jnp.float32
    )
    sigmoid = jax.nn.sigmoid(pre_act)
    output_feat = (pre_act * sigmoid).astype(jnp.bfloat16)
    grad_pre = (
        grad_output.astype(jnp.float32) * sigmoid * (1.0 + pre_act * (1.0 - sigmoid))
    ).astype(jnp.bfloat16)
    weight_part = lax.dot_general(
        aggregate, grad_pre, (((1,), (1,)), ((), ())), preferred_element_type=jnp.float32
    )
    grad_full = gather(grad_pre, "col")
    grad_agg = jnp.dot(weight, grad_full, preferred_element_type=jnp.float32).astype(jnp.bfloat16)
    input_part = backward_block(values, slots, live_count, grad_agg, col_tiles, loop_count)
    grad_input = scatter_sum(input_part.astype(jnp.bfloat16), "row")
    weight_share = scatter_sum(weight_part.astype(jnp.bfloat16), "row")
    node_total = grad_output.shape[1] * lax.axis_size("row")
    return (output_feat, weight_share * node_total ** (-0.5), grad_input)


def solution(mesh):
    in_specs = (
        P("row", "col"),
        P(),
        P("row", "col", None, None, None),
        P("row", "col", None),
        P("row", "col"),
        P("col", "row"),
    )
    out_specs = (P("col", "row"), P("row", "col"), P("row", "col"))
    R, C = mesh.shape["row"], mesh.shape["col"]

    def device(x, w, tv, slots, count, go):
        if R % 2 == 0 and go.shape[1] % (C * tv.shape[-1]) == 0 and x.shape[0] % 16 == 0:
            return fused_device(R, C, x, w, tv, slots, count, go)
        return per_device(x, w, tv, slots, count, go)

    return jax.shard_map(
        device, mesh=mesh, in_specs=in_specs, out_specs=out_specs, check_vma=False
    )
```

```python
import functools

import jax
import jax.numpy as jnp
from jax import lax
from jax.experimental import pallas as pl
from jax.experimental.pallas import tpu as pltpu
from jax.sharding import PartitionSpec as P

F32, BF16 = jnp.float32, jnp.bfloat16


def fused(
    R, C, T, x_hbm, w_hbm, tv_hbm, slots_ref, count_ref, go_hbm, of_ref, wg_ref, gi_ref,
    x_ref, w_ref, go_ref, lsem,
    tv_all, xf, pout, prx, agg_s, agg_full, go_full, of_s, of_rx, w_s, w_rx, w2_s, w2_rx,
    ga_s, ga_rx, ga_all,
    sdir, sfwd, rtv, sgo, rgo, szr, rzr, sa, ra, sof, rof, swz, rwz, swr, rwr, sg, rg, sgz, rgz, sgl,
):
    L = tv_hbm.shape[1]
    FR, NB = x_ref.shape
    FC, NR = go_ref.shape
    F = w_ref.shape[0]
    RT, CT, SH = NR // L, NB // L, NR // C
    per = SH // L
    mi, mj = lax.axis_index("row"), lax.axis_index("col")
    sib = mi + 1 - 2 * lax.rem(mi, 2)
    half = R // 2

    def rowp(p):
        return {"row": p}

    def colp(p):
        return {"col": p}

    def rcopy(src, dst, ss, rs, dev):
        return pltpu.make_async_remote_copy(
            src_ref=src, dst_ref=dst, send_sem=ss, recv_sem=rs, device_id=dev,
            device_id_type=pl.DeviceIdType.MESH,
        )

    def rows(d):
        return lax.rem(mi + d, R)

    def cols(d):
        return lax.rem(mj + d, C)

    loads = [
        pltpu.make_async_copy(tv_hbm, tv_all.at[mi, 0 : T * L], lsem.at[0]),
        pltpu.make_async_copy(go_hbm, go_ref, lsem.at[1]),
        pltpu.make_async_copy(x_hbm, x_ref, lsem.at[2]),
        pltpu.make_async_copy(w_hbm, w_ref, lsem.at[3]),
    ]
    for load in loads:
        load.start()

    barrier = pltpu.get_barrier_semaphore()
    for d in range(1, R):
        pl.semaphore_signal(barrier, inc=1, device_id=rowp(rows(d)), device_id_type=pl.DeviceIdType.MESH)
    for d in range(1, C):
        pl.semaphore_signal(barrier, inc=1, device_id=colp(cols(d)), device_id_type=pl.DeviceIdType.MESH)

    count = count_ref[0, 0]
    lines = []
    for t in range(T):
        lines.append(jnp.full((1, L), lax.rem(slots_ref[0, 0, t], CT), jnp.int32))
    for t in range(T):
        home = jnp.where(t < count, lax.div(slots_ref[0, 0, t], CT), RT)
        lines.append(jnp.full((1, L), home, jnp.int32))
    tv_all[mi, T * L : T * L + 2 * T, :] = jnp.concatenate(lines, axis=0).astype(F32).astype(BF16)
    pl.semaphore_wait(barrier, R + C - 2)
    loads[0].wait()
    loads[1].wait()

    for m in range(1, half):
        rcopy(tv_all.at[mi], tv_all.at[mi], sdir.at[m], rtv.at[mi], rowp(rows(2 * m))).start()
    for d in range(1, C):
        rcopy(
            go_ref.at[:, pl.ds(pl.multiple_of(cols(d) * SH, SH), SH)],
            go_full.at[mj], sgo.at[d], rgo.at[mj], colp(cols(d)),
        ).start()
    go_full[mj] = go_ref[:, pl.ds(pl.multiple_of(mj * SH, SH), SH)]

    loads[2].wait()
    xf[...] = x_ref[...].astype(F32)

    def forward(b):
        info = tv_all[b, T * L : T * L + 2 * T, :].astype(F32)
        prods = []
        for t in range(T):
            colv = jnp.broadcast_to(info[t : t + 1, :], (FR, L))
            pick = jnp.zeros((FR, L), F32)
            for c in range(CT):
                pick = jnp.where(colv == c, xf[:, c * L : (c + 1) * L], pick)
            prods.append(
                lax.dot_general(
                    pick.astype(BF16), tv_all[b, t * L : (t + 1) * L, :],
                    (((1,), (1,)), ((), ())), preferred_element_type=F32,
                )
            )
        for k in range(RT):
            acc = jnp.zeros((FR, L), F32)
            for t in range(T):
                rowv = jnp.broadcast_to(info[T + t : T + t + 1, :], (FR, L))
                acc = acc + jnp.where(rowv == k, prods[t], 0.0)
            pout[k // per, b, :, (k % per) * L : (k % per + 1) * L] = acc.astype(BF16)
        for d in range(1, C):
            rcopy(
                pout.at[cols(d), b], prx.at[mj, b], szr.at[b, d], rzr.at[b, mj], colp(cols(d))
            ).start()

    def wait_tv(b):
        rcopy(tv_all.at[b], tv_all.at[b], sfwd.at[0], rtv.at[b], rowp(sib)).wait_recv()

    def gather_step(m, carry):
        p, q = rows(2 * m), lax.rem(sib + 2 * m, R)

        @pl.when(m > 0)
        def _():
            wait_tv(p)

        rcopy(tv_all.at[p], tv_all.at[p], sfwd.at[m], rtv.at[p], rowp(sib)).start()

        def one(h, carry):
            b = jnp.where(h == 0, p, q)

            @pl.when(h == 1)
            def _():
                wait_tv(q)

            forward(b)
            return carry

        return lax.fori_loop(0, 2, one, carry)

    lax.fori_loop(0, half, gather_step, 0)

    def reduce_step(n, carry):
        m, h = lax.div(n, 2), lax.rem(n, 2)
        b = lax.rem(jnp.where(h == 0, mi, sib) + 2 * m, R)
        total = pout[mj, b].astype(F32)
        for d in range(1, C):
            rcopy(pout.at[cols(d), b], prx.at[cols(d), b], szr.at[b, d], rzr.at[b, cols(d)], colp(cols(d))).wait_recv()
            total = total + prx[cols(d), b].astype(F32)
        agg_s[b] = total.astype(BF16)

        @pl.when(b == mi)
        def _():
            agg_full[mi] = agg_s[mi]

        @pl.when(b != mi)
        def _():
            rcopy(agg_s.at[b], agg_full.at[mi], sa.at[b], ra.at[mi], rowp(b)).start()

        return carry

    lax.fori_loop(0, R, reduce_step, 0)

    for d in range(1, C):
        rcopy(go_full.at[cols(d)], go_full.at[cols(d)], sgo.at[d], rgo.at[cols(d)], colp(cols(d))).wait_recv()
    for d in range(1, R):
        p = rows(d)
        rcopy(agg_s.at[p], agg_full.at[p], sa.at[p], ra.at[p], rowp(p)).wait_recv()

    loads[3].wait()
    agg = agg_full[...].reshape(F, SH)
    pre = lax.dot_general(w_ref[...], agg, (((0,), (0,)), ((), ())), preferred_element_type=F32)
    s = 1.0 / (1.0 + jnp.exp(-pre))
    gp = (go_full[...].reshape(F, SH).astype(F32) * s * (1.0 + pre * (1.0 - s))).astype(BF16)
    ga_s[...] = jnp.dot(w_ref[...], gp, preferred_element_type=F32).astype(BF16).reshape(R, FR, SH)
    for d in range(1, R):
        p = rows(d)
        rcopy(ga_s.at[p], ga_rx.at[mi], sg.at[p], rg.at[mi], rowp(p)).start()
    of_s[...] = (pre * s).astype(BF16).reshape(C, FC, SH)
    ga_rx[mi] = ga_s[mi]

    def hop(q, b, way):
        sems = sgz if way > 0 else sgl
        return rcopy(ga_all.at[q, b], ga_all.at[q, b], sems.at[b, q], rgz.at[b, q], colp(mj + way))

    def pass_on(q, b):
        @pl.when((q <= mj) & (mj < C - 1))
        def _():
            hop(q, b, 1).start()

        @pl.when((q >= mj) & (mj > 0))
        def _():
            hop(q, b, -1).start()

    def relay(n, carry):
        b = rows(lax.rem(n, R))
        d = lax.div(n, R) + 1

        @pl.when(mj >= d)
        def _():
            hop(mj - d, b, -1).wait_recv()
            pass_on(mj - d, b)

        @pl.when(mj + d < C)
        def _():
            hop(mj + d, b, 1).wait_recv()
            pass_on(mj + d, b)

        return carry

    def spread(n, carry):
        p = rows(n)

        @pl.when(n > 0)
        def _():
            rcopy(ga_s.at[p], ga_rx.at[p], sg.at[p], rg.at[p], rowp(p)).wait_recv()

        ga_all[mj, p] = ga_rx[p]
        pass_on(mj, p)
        return carry

    lax.fori_loop(0, R, spread, 0)

    w_s[...] = lax.dot_general(
        agg, gp, (((1,), (1,)), ((), ())), preferred_element_type=F32
    ).astype(BF16).reshape(R, FR, F)
    for d in range(1, R):
        p = rows(d)
        rcopy(w_s.at[p], w_rx.at[mi], swr.at[p], rwr.at[mi], rowp(p)).start()
    for d in range(1, C):
        q = cols(d)
        rcopy(of_s.at[q], of_rx.at[mj], sof.at[d], rof.at[mj], colp(q)).start()
    of_rx[mj] = of_s[mj]

    total = w_s[mi].astype(F32)
    for d in range(1, R):
        p = rows(d)
        rcopy(w_s.at[p], w_rx.at[p], swr.at[p], rwr.at[p], rowp(p)).wait_recv()
        total = total + w_rx[p].astype(F32)
    for j in range(C):
        w2_s[j] = total[:, j * FC : (j + 1) * FC].astype(BF16)
    for d in range(1, C):
        q = cols(d)
        rcopy(w2_s.at[q], w2_rx.at[mj], swz.at[d], rwz.at[mj], colp(q)).start()

    gi_ref[...] = jnp.zeros_like(gi_ref)

    def backward(n, carry):
        relay(n + R * (C - 2), carry)
        b = rows(n)
        info = tv_all[b, T * L : T * L + 2 * T, :].astype(F32)
        prods = []
        for t in range(T):
            rowv = jnp.broadcast_to(info[T + t : T + t + 1, :], (FR, L))
            pick = jnp.zeros((FR, L), F32)
            for k in range(RT):
                part = ga_all[k // per, b, :, (k % per) * L : (k % per + 1) * L].astype(F32)
                pick = jnp.where(rowv == k, part, pick)
            prods.append(
                jnp.dot(pick.astype(BF16), tv_all[b, t * L : (t + 1) * L, :], preferred_element_type=F32)
            )
        for c in range(CT):
            acc = gi_ref[:, c * L : (c + 1) * L]
            for t in range(T):
                colv = jnp.broadcast_to(info[t : t + 1, :], (FR, L))
                acc = acc + jnp.where(colv == c, prods[t], 0.0)
            gi_ref[:, c * L : (c + 1) * L] = acc
        return carry

    lax.fori_loop(0, R * (C - 2), relay, 0)
    lax.fori_loop(0, R, backward, 0)

    for d in range(1, C):
        q = cols(d)
        rcopy(of_s.at[q], of_rx.at[q], sof.at[d], rof.at[q], colp(q)).wait_recv()
    for j in range(C):
        of_ref[:, j * SH : (j + 1) * SH] = of_rx[j]
    total = w2_s[mj].astype(F32)
    for d in range(1, C):
        q = cols(d)
        rcopy(w2_s.at[q], w2_rx.at[q], swz.at[d], rwz.at[q], colp(q)).wait_recv()
        total = total + w2_rx[q].astype(F32)
    wg_ref[...] = total * (NR * R) ** -0.5

    for m in range(1, half):
        rcopy(tv_all.at[mi], tv_all.at[mi], sdir.at[m], rtv.at[mi], rowp(rows(2 * m))).wait_send()
    for m in range(half):
        rcopy(tv_all.at[mi], tv_all.at[mi], sfwd.at[m], rtv.at[mi], rowp(sib)).wait_send()
    for d in range(1, C):
        q = cols(d)
        rcopy(go_full.at[mj], go_full.at[mj], sgo.at[d], rgo.at[mj], colp(q)).wait_send()
        rcopy(w2_s.at[q], w2_rx.at[mj], swz.at[d], rwz.at[mj], colp(q)).wait_send()
        rcopy(of_s.at[q], of_rx.at[mj], sof.at[d], rof.at[mj], colp(q)).wait_send()

    def drain(n, carry):
        p = rows(n)
        for d in range(1, C):
            q = cols(d)
            rcopy(pout.at[q, p], prx.at[mj, p], szr.at[p, d], rzr.at[p, mj], colp(q)).wait_send()

        for q in range(C):
            @pl.when((q <= mj) & (mj < C - 1))
            def _(q=q):
                hop(q, p, 1).wait_send()

            @pl.when((q >= mj) & (mj > 0))
            def _(q=q):
                hop(q, p, -1).wait_send()

        @pl.when(n > 0)
        def _():
            rcopy(agg_s.at[p], agg_full.at[mi], sa.at[p], ra.at[mi], rowp(p)).wait_send()
            rcopy(ga_s.at[p], ga_rx.at[mi], sg.at[p], rg.at[mi], rowp(p)).wait_send()
            rcopy(w_s.at[p], w_rx.at[mi], swr.at[p], rwr.at[mi], rowp(p)).wait_send()

        return carry

    lax.fori_loop(0, R, drain, 0)


def fused_device(R, C, x, w, tv, slots, count, go):
    T, L = tv.shape[2], tv.shape[3]
    FR, NB = x.shape
    FC, NR = go.shape
    F, SH = w.shape[0], NR // C
    vm, dma = pltpu.VMEM, pltpu.SemaphoreType.DMA
    scratch = [
        vm((FR, NB), BF16), vm((F, F), BF16), vm((FC, NR), BF16), dma((4,)),
        vm((R, T * L + 2 * T, L), BF16), vm((FR, NB), F32),
        vm((C, R, FR, SH), BF16), vm((C, R, FR, SH), BF16),
        vm((R, FR, SH), BF16), vm((R, FR, SH), BF16), vm((C, FC, SH), BF16),
        vm((C, FC, SH), BF16), vm((C, FC, SH), BF16),
        vm((R, FR, F), BF16), vm((R, FR, F), BF16),
        vm((C, FR, FC), BF16), vm((C, FR, FC), BF16),
        vm((R, FR, SH), BF16), vm((R, FR, SH), BF16), vm((C, R, FR, SH), BF16),
        dma((R // 2,)), dma((R // 2,)), dma((R,)), dma((C,)), dma((C,)),
        dma((R, C)), dma((R, C)), dma((R,)), dma((R,)), dma((C,)), dma((C,)),
        dma((C,)), dma((C,)), dma((R,)), dma((R,)), dma((R,)), dma((R,)), dma((R, C)), dma((R, C)), dma((R, C)),
    ]
    vmem, smem = pl.BlockSpec(memory_space=pltpu.VMEM), pl.BlockSpec(memory_space=pltpu.SMEM)
    hbm = pl.BlockSpec(memory_space=pltpu.HBM)
    return pl.pallas_call(
        functools.partial(fused, R, C, T),
        out_shape=(
            jax.ShapeDtypeStruct((FC, NR), BF16),
            jax.ShapeDtypeStruct((FR, FC), F32),
            jax.ShapeDtypeStruct((FR, NB), F32),
        ),
        in_specs=[hbm, hbm, hbm, smem, smem, hbm],
        out_specs=(vmem, vmem, vmem),
        scratch_shapes=scratch,
        compiler_params=pltpu.CompilerParams(
            collective_id=0, has_side_effects=True, vmem_limit_bytes=60 * 1024 * 1024
        ),
    )(x, w, tv.reshape(T * L, L), slots, count, go)


def gather(x, axis):
    n = lax.axis_size(axis)
    spread = jnp.broadcast_to(x[None], (n,) + x.shape)
    return lax.all_to_all(spread, axis, 0, 0).reshape((n * x.shape[0],) + x.shape[1:])


def scatter_sum(x, axis):
    n = lax.axis_size(axis)
    parts = lax.all_to_all(x.reshape((n, x.shape[0] // n) + x.shape[1:]), axis, 0, 0)
    return jnp.sum(parts.astype(F32), axis=0)


def pick_blocks(blocks, index):
    chosen = index[:, None] == jnp.arange(blocks.shape[1], dtype=jnp.int32)[None, :]
    return jnp.einsum("fkc,tk->ftc", blocks, chosen.astype(blocks.dtype))


def forward_block(values, slots, live_count, columns, row_tiles, loop_count):
    channels = columns.shape[0]
    tile_len = values.shape[-1]
    col_tiles = columns.shape[1] // tile_len
    blocks = columns.reshape(channels, col_tiles, tile_len)

    def forward_add_group(group_idx, running):
        first_tile = group_idx * 8
        is_live = first_tile + jnp.arange(8, dtype=jnp.int32) < live_count
        picked = pick_blocks(blocks, slots % col_tiles)
        products = jnp.einsum("ftc,trc->tfr", picked, values, preferred_element_type=jnp.float32)
        target = (
            (slots // col_tiles)[:, None] == jnp.arange(row_tiles, dtype=jnp.int32)[None, :]
        ) & is_live[:, None]
        return running + jnp.einsum(
            "tfr,tk->fkr", products, target.astype(jnp.float32), precision=lax.Precision.HIGHEST
        )

    running = lax.fori_loop(
        0, loop_count, forward_add_group, jnp.zeros((channels, row_tiles, tile_len), jnp.float32)
    )
    return running.reshape(channels, row_tiles * tile_len)


def backward_block(values, slots, live_count, rows, col_tiles, loop_count):
    channels = rows.shape[0]
    tile_len = values.shape[-1]
    row_tiles = rows.shape[1] // tile_len
    blocks = rows.reshape(channels, row_tiles, tile_len)

    def backward_add_group(group_idx, running):
        first_tile = group_idx * 8
        is_live = first_tile + jnp.arange(8, dtype=jnp.int32) < live_count
        picked = pick_blocks(blocks, slots // col_tiles)
        products = jnp.einsum("ftr,trc->tfc", picked, values, preferred_element_type=jnp.float32)
        target = (
            (slots % col_tiles)[:, None] == jnp.arange(col_tiles, dtype=jnp.int32)[None, :]
        ) & is_live[:, None]
        return running + jnp.einsum(
            "tfc,tk->fkc", products, target.astype(jnp.float32), precision=lax.Precision.HIGHEST
        )

    running = lax.fori_loop(
        0, loop_count, backward_add_group, jnp.zeros((channels, col_tiles, tile_len), jnp.float32)
    )
    return running.reshape(channels, col_tiles * tile_len)


def per_device(input_feat, weight, tile_values, tile_slots, tile_count, grad_output):
    values = tile_values[0, 0]
    slots = tile_slots[0, 0]
    live_count = tile_count[0, 0]
    tile_len = values.shape[-1]
    row_tiles = grad_output.shape[1] // tile_len
    col_tiles = input_feat.shape[1] // tile_len
    loop_count = values.shape[0] // 8
    partial_agg = forward_block(
        values,
        slots,
        live_count,
        gather(input_feat, "row"),
        row_tiles,
        loop_count,
    )
    aggregate = gather(scatter_sum(partial_agg.astype(jnp.bfloat16), "col").astype(jnp.bfloat16), "col")
    out_width = weight.shape[1] // lax.axis_size("col")
    weight_cols = lax.dynamic_slice_in_dim(weight, lax.axis_index("col") * out_width, out_width, 1)
    pre_act = lax.dot_general(
        weight_cols, aggregate, (((0,), (0,)), ((), ())), preferred_element_type=jnp.float32
    )
    sigmoid = jax.nn.sigmoid(pre_act)
    output_feat = (pre_act * sigmoid).astype(jnp.bfloat16)
    grad_pre = (
        grad_output.astype(jnp.float32) * sigmoid * (1.0 + pre_act * (1.0 - sigmoid))
    ).astype(jnp.bfloat16)
    weight_part = lax.dot_general(
        aggregate, grad_pre, (((1,), (1,)), ((), ())), preferred_element_type=jnp.float32
    )
    grad_full = gather(grad_pre, "col")
    grad_agg = jnp.dot(weight, grad_full, preferred_element_type=jnp.float32).astype(jnp.bfloat16)
    input_part = backward_block(values, slots, live_count, grad_agg, col_tiles, loop_count)
    grad_input = scatter_sum(input_part.astype(jnp.bfloat16), "row")
    weight_share = scatter_sum(weight_part.astype(jnp.bfloat16), "row")
    node_total = grad_output.shape[1] * lax.axis_size("row")
    return (output_feat, weight_share * node_total ** (-0.5), grad_input)


def solution(mesh):
    in_specs = (
        P("row", "col"),
        P(),
        P("row", "col", None, None, None),
        P("row", "col", None),
        P("row", "col"),
        P("col", "row"),
    )
    out_specs = (P("col", "row"), P("row", "col"), P("row", "col"))
    R, C = mesh.shape["row"], mesh.shape["col"]

    def device(x, w, tv, slots, count, go):
        if R % 2 == 0 and go.shape[1] % (C * tv.shape[-1]) == 0 and x.shape[0] % 16 == 0:
            return fused_device(R, C, x, w, tv, slots, count, go)
        return per_device(x, w, tv, slots, count, go)

    return jax.shard_map(
        device, mesh=mesh, in_specs=in_specs, out_specs=out_specs, check_vma=False
    )
```

```python
import functools

import jax
import jax.numpy as jnp
from jax import lax
from jax.experimental import pallas as pl
from jax.experimental.pallas import tpu as pltpu
from jax.sharding import PartitionSpec as P

F32, BF16 = jnp.float32, jnp.bfloat16


def fused(
    R, C, T, x_hbm, w_hbm, tv_hbm, slots_ref, count_ref, go_hbm, of_ref, wg_ref, gi_ref,
    x_ref, w_ref, go_ref, lsem,
    tv_all, xf, pout, prx, agg_s, agg_full, go_full, of_s, of_rx, w_s, w_rx, w2_s, w2_rx,
    ga_s, ga_rx, ga_all,
    sdir, sfwd, rtv, sgo, rgo, szr, rzr, sa, ra, sof, rof, swz, rwz, swr, rwr, sg, rg, sgz, rgz, sgl,
):
    L = tv_hbm.shape[1]
    FR, NB = x_ref.shape
    FC, NR = go_ref.shape
    F = w_ref.shape[0]
    RT, CT, SH = NR // L, NB // L, NR // C
    per = SH // L
    mi, mj = lax.axis_index("row"), lax.axis_index("col")
    sib = mi + 1 - 2 * lax.rem(mi, 2)
    half = R // 2

    def rowp(p):
        return {"row": p}

    def colp(p):
        return {"col": p}

    def rcopy(src, dst, ss, rs, dev):
        return pltpu.make_async_remote_copy(
            src_ref=src, dst_ref=dst, send_sem=ss, recv_sem=rs, device_id=dev,
            device_id_type=pl.DeviceIdType.MESH,
        )

    def rows(d):
        return lax.rem(mi + d, R)

    def cols(d):
        return lax.rem(mj + d, C)

    loads = [
        pltpu.make_async_copy(tv_hbm, tv_all.at[mi, 0 : T * L], lsem.at[0]),
        pltpu.make_async_copy(go_hbm, go_ref, lsem.at[1]),
        pltpu.make_async_copy(x_hbm, x_ref, lsem.at[2]),
        pltpu.make_async_copy(w_hbm, w_ref, lsem.at[3]),
    ]
    for load in loads:
        load.start()

    barrier = pltpu.get_barrier_semaphore()
    for d in range(1, R):
        pl.semaphore_signal(barrier, inc=1, device_id=rowp(rows(d)), device_id_type=pl.DeviceIdType.MESH)
    for d in range(1, C):
        pl.semaphore_signal(barrier, inc=1, device_id=colp(cols(d)), device_id_type=pl.DeviceIdType.MESH)

    count = count_ref[0, 0]
    lines = []
    for t in range(T):
        lines.append(jnp.full((1, L), lax.rem(slots_ref[0, 0, t], CT), jnp.int32))
    for t in range(T):
        home = jnp.where(t < count, lax.div(slots_ref[0, 0, t], CT), RT)
        lines.append(jnp.full((1, L), home, jnp.int32))
    tv_all[mi, T * L : T * L + 2 * T, :] = jnp.concatenate(lines, axis=0).astype(F32).astype(BF16)
    pl.semaphore_wait(barrier, R + C - 2)
    loads[0].wait()
    loads[1].wait()

    for m in range(1, half):
        rcopy(tv_all.at[mi], tv_all.at[mi], sdir.at[m], rtv.at[mi], rowp(rows(2 * m))).start()
    for d in range(1, C):
        rcopy(
            go_ref.at[:, pl.ds(pl.multiple_of(cols(d) * SH, SH), SH)],
            go_full.at[mj], sgo.at[d], rgo.at[mj], colp(cols(d)),
        ).start()
    go_full[mj] = go_ref[:, pl.ds(pl.multiple_of(mj * SH, SH), SH)]

    loads[2].wait()
    xf[...] = x_ref[...].astype(F32)

    def forward(b):
        info = tv_all[b, T * L : T * L + 2 * T, :].astype(F32)
        prods = []
        for t in range(T):
            colv = jnp.broadcast_to(info[t : t + 1, :], (FR, L))
            pick = jnp.zeros((FR, L), F32)
            for c in range(CT):
                pick = jnp.where(colv == c, xf[:, c * L : (c + 1) * L], pick)
            prods.append(
                lax.dot_general(
                    pick.astype(BF16), tv_all[b, t * L : (t + 1) * L, :],
                    (((1,), (1,)), ((), ())), preferred_element_type=F32,
                )
            )
        for k in range(RT):
            acc = jnp.zeros((FR, L), F32)
            for t in range(T):
                rowv = jnp.broadcast_to(info[T + t : T + t + 1, :], (FR, L))
                acc = acc + jnp.where(rowv == k, prods[t], 0.0)
            pout[k // per, b, :, (k % per) * L : (k % per + 1) * L] = acc.astype(BF16)
        for d in range(1, C):
            rcopy(
                pout.at[cols(d), b], prx.at[mj, b], szr.at[b, d], rzr.at[b, mj], colp(cols(d))
            ).start()

    def wait_tv(b):
        rcopy(tv_all.at[b], tv_all.at[b], sfwd.at[0], rtv.at[b], rowp(sib)).wait_recv()

    def gather_step(m, carry):
        p, q = rows(2 * m), lax.rem(sib + 2 * m, R)

        @pl.when(m > 0)
        def _():
            wait_tv(p)

        rcopy(tv_all.at[p], tv_all.at[p], sfwd.at[m], rtv.at[p], rowp(sib)).start()

        def one(h, carry):
            b = jnp.where(h == 0, p, q)

            @pl.when(h == 1)
            def _():
                wait_tv(q)

            forward(b)
            return carry

        return lax.fori_loop(0, 2, one, carry)

    lax.fori_loop(0, half, gather_step, 0)

    def reduce_step(n, carry):
        m, h = lax.div(n, 2), lax.rem(n, 2)
        b = lax.rem(jnp.where(h == 0, mi, sib) + 2 * m, R)
        total = pout[mj, b].astype(F32)
        for d in range(1, C):
            rcopy(pout.at[cols(d), b], prx.at[cols(d), b], szr.at[b, d], rzr.at[b, cols(d)], colp(cols(d))).wait_recv()
            total = total + prx[cols(d), b].astype(F32)
        agg_s[b] = total.astype(BF16)

        @pl.when(b == mi)
        def _():
            agg_full[mi] = agg_s[mi]

        @pl.when(b != mi)
        def _():
            rcopy(agg_s.at[b], agg_full.at[mi], sa.at[b], ra.at[mi], rowp(b)).start()

        return carry

    lax.fori_loop(0, R, reduce_step, 0)

    for d in range(1, C):
        rcopy(go_full.at[cols(d)], go_full.at[cols(d)], sgo.at[d], rgo.at[cols(d)], colp(cols(d))).wait_recv()
    for d in range(1, R):
        p = rows(d)
        rcopy(agg_s.at[p], agg_full.at[p], sa.at[p], ra.at[p], rowp(p)).wait_recv()

    loads[3].wait()
    agg = agg_full[...].reshape(F, SH)
    pre = lax.dot_general(w_ref[...], agg, (((0,), (0,)), ((), ())), preferred_element_type=F32)
    s = 1.0 / (1.0 + jnp.exp(-pre))
    of_s[...] = (pre * s).astype(BF16).reshape(C, FC, SH)
    for d in range(1, C):
        q = cols(d)
        rcopy(of_s.at[q], of_rx.at[mj], sof.at[d], rof.at[mj], colp(q)).start()
    gp = (go_full[...].reshape(F, SH).astype(F32) * s * (1.0 + pre * (1.0 - s))).astype(BF16)
    ga_s[...] = jnp.dot(w_ref[...], gp, preferred_element_type=F32).astype(BF16).reshape(R, FR, SH)
    for d in range(1, R):
        p = rows(d)
        rcopy(ga_s.at[p], ga_rx.at[mi], sg.at[p], rg.at[mi], rowp(p)).start()
    ga_rx[mi] = ga_s[mi]

    def hop(q, b, way):
        sems = sgz if way > 0 else sgl
        return rcopy(ga_all.at[q, b], ga_all.at[q, b], sems.at[b, q], rgz.at[b, q], colp(mj + way))

    def pass_on(q, b):
        @pl.when((q <= mj) & (mj < C - 1))
        def _():
            hop(q, b, 1).start()

        @pl.when((q >= mj) & (mj > 0))
        def _():
            hop(q, b, -1).start()

    def relay(n, carry):
        b = rows(lax.rem(n, R))
        d = lax.div(n, R) + 1

        @pl.when(mj >= d)
        def _():
            hop(mj - d, b, -1).wait_recv()
            pass_on(mj - d, b)

        @pl.when(mj + d < C)
        def _():
            hop(mj + d, b, 1).wait_recv()
            pass_on(mj + d, b)

        return carry

    def spread(n, carry):
        p = rows(n)

        @pl.when(n > 0)
        def _():
            rcopy(ga_s.at[p], ga_rx.at[p], sg.at[p], rg.at[p], rowp(p)).wait_recv()

        ga_all[mj, p] = ga_rx[p]
        pass_on(mj, p)
        return carry

    lax.fori_loop(0, R, spread, 0)

    w_s[...] = lax.dot_general(
        agg, gp, (((1,), (1,)), ((), ())), preferred_element_type=F32
    ).astype(BF16).reshape(R, FR, F)
    for d in range(1, R):
        p = rows(d)
        rcopy(w_s.at[p], w_rx.at[mi], swr.at[p], rwr.at[mi], rowp(p)).start()
    of_rx[mj] = of_s[mj]

    total = w_s[mi].astype(F32)
    for d in range(1, R):
        p = rows(d)
        rcopy(w_s.at[p], w_rx.at[p], swr.at[p], rwr.at[p], rowp(p)).wait_recv()
        total = total + w_rx[p].astype(F32)
    for j in range(C):
        w2_s[j] = total[:, j * FC : (j + 1) * FC].astype(BF16)
    for d in range(1, C):
        q = cols(d)
        rcopy(w2_s.at[q], w2_rx.at[mj], swz.at[d], rwz.at[mj], colp(q)).start()

    gi_ref[...] = jnp.zeros_like(gi_ref)

    def backward(n, carry):
        relay(n + R * (C - 2), carry)
        b = rows(n)
        info = tv_all[b, T * L : T * L + 2 * T, :].astype(F32)
        prods = []
        for t in range(T):
            rowv = jnp.broadcast_to(info[T + t : T + t + 1, :], (FR, L))
            pick = jnp.zeros((FR, L), F32)
            for k in range(RT):
                part = ga_all[k // per, b, :, (k % per) * L : (k % per + 1) * L].astype(F32)
                pick = jnp.where(rowv == k, part, pick)
            prods.append(
                jnp.dot(pick.astype(BF16), tv_all[b, t * L : (t + 1) * L, :], preferred_element_type=F32)
            )
        for c in range(CT):
            acc = gi_ref[:, c * L : (c + 1) * L]
            for t in range(T):
                colv = jnp.broadcast_to(info[t : t + 1, :], (FR, L))
                acc = acc + jnp.where(colv == c, prods[t], 0.0)
            gi_ref[:, c * L : (c + 1) * L] = acc
        return carry

    lax.fori_loop(0, R * (C - 2), relay, 0)
    lax.fori_loop(0, R, backward, 0)

    for d in range(1, C):
        q = cols(d)
        rcopy(of_s.at[q], of_rx.at[q], sof.at[d], rof.at[q], colp(q)).wait_recv()
    for j in range(C):
        of_ref[:, j * SH : (j + 1) * SH] = of_rx[j]
    total = w2_s[mj].astype(F32)
    for d in range(1, C):
        q = cols(d)
        rcopy(w2_s.at[q], w2_rx.at[q], swz.at[d], rwz.at[q], colp(q)).wait_recv()
        total = total + w2_rx[q].astype(F32)
    wg_ref[...] = total * (NR * R) ** -0.5

    for m in range(1, half):
        rcopy(tv_all.at[mi], tv_all.at[mi], sdir.at[m], rtv.at[mi], rowp(rows(2 * m))).wait_send()
    for m in range(half):
        rcopy(tv_all.at[mi], tv_all.at[mi], sfwd.at[m], rtv.at[mi], rowp(sib)).wait_send()
    for d in range(1, C):
        q = cols(d)
        rcopy(go_full.at[mj], go_full.at[mj], sgo.at[d], rgo.at[mj], colp(q)).wait_send()
        rcopy(w2_s.at[q], w2_rx.at[mj], swz.at[d], rwz.at[mj], colp(q)).wait_send()
        rcopy(of_s.at[q], of_rx.at[mj], sof.at[d], rof.at[mj], colp(q)).wait_send()

    def drain(n, carry):
        p = rows(n)
        for d in range(1, C):
            q = cols(d)
            rcopy(pout.at[q, p], prx.at[mj, p], szr.at[p, d], rzr.at[p, mj], colp(q)).wait_send()

        for q in range(C):
            @pl.when((q <= mj) & (mj < C - 1))
            def _(q=q):
                hop(q, p, 1).wait_send()

            @pl.when((q >= mj) & (mj > 0))
            def _(q=q):
                hop(q, p, -1).wait_send()

        @pl.when(n > 0)
        def _():
            rcopy(agg_s.at[p], agg_full.at[mi], sa.at[p], ra.at[mi], rowp(p)).wait_send()
            rcopy(ga_s.at[p], ga_rx.at[mi], sg.at[p], rg.at[mi], rowp(p)).wait_send()
            rcopy(w_s.at[p], w_rx.at[mi], swr.at[p], rwr.at[mi], rowp(p)).wait_send()

        return carry

    lax.fori_loop(0, R, drain, 0)


def fused_device(R, C, x, w, tv, slots, count, go):
    T, L = tv.shape[2], tv.shape[3]
    FR, NB = x.shape
    FC, NR = go.shape
    F, SH = w.shape[0], NR // C
    vm, dma = pltpu.VMEM, pltpu.SemaphoreType.DMA
    scratch = [
        vm((FR, NB), BF16), vm((F, F), BF16), vm((FC, NR), BF16), dma((4,)),
        vm((R, T * L + 2 * T, L), BF16), vm((FR, NB), F32),
        vm((C, R, FR, SH), BF16), vm((C, R, FR, SH), BF16),
        vm((R, FR, SH), BF16), vm((R, FR, SH), BF16), vm((C, FC, SH), BF16),
        vm((C, FC, SH), BF16), vm((C, FC, SH), BF16),
        vm((R, FR, F), BF16), vm((R, FR, F), BF16),
        vm((C, FR, FC), BF16), vm((C, FR, FC), BF16),
        vm((R, FR, SH), BF16), vm((R, FR, SH), BF16), vm((C, R, FR, SH), BF16),
        dma((R // 2,)), dma((R // 2,)), dma((R,)), dma((C,)), dma((C,)),
        dma((R, C)), dma((R, C)), dma((R,)), dma((R,)), dma((C,)), dma((C,)),
        dma((C,)), dma((C,)), dma((R,)), dma((R,)), dma((R,)), dma((R,)), dma((R, C)), dma((R, C)), dma((R, C)),
    ]
    vmem, smem = pl.BlockSpec(memory_space=pltpu.VMEM), pl.BlockSpec(memory_space=pltpu.SMEM)
    hbm = pl.BlockSpec(memory_space=pltpu.HBM)
    return pl.pallas_call(
        functools.partial(fused, R, C, T),
        out_shape=(
            jax.ShapeDtypeStruct((FC, NR), BF16),
            jax.ShapeDtypeStruct((FR, FC), F32),
            jax.ShapeDtypeStruct((FR, NB), F32),
        ),
        in_specs=[hbm, hbm, hbm, smem, smem, hbm],
        out_specs=(vmem, vmem, vmem),
        scratch_shapes=scratch,
        compiler_params=pltpu.CompilerParams(
            collective_id=0, has_side_effects=True, vmem_limit_bytes=60 * 1024 * 1024
        ),
    )(x, w, tv.reshape(T * L, L), slots, count, go)


def gather(x, axis):
    n = lax.axis_size(axis)
    spread = jnp.broadcast_to(x[None], (n,) + x.shape)
    return lax.all_to_all(spread, axis, 0, 0).reshape((n * x.shape[0],) + x.shape[1:])


def scatter_sum(x, axis):
    n = lax.axis_size(axis)
    parts = lax.all_to_all(x.reshape((n, x.shape[0] // n) + x.shape[1:]), axis, 0, 0)
    return jnp.sum(parts.astype(F32), axis=0)


def pick_blocks(blocks, index):
    chosen = index[:, None] == jnp.arange(blocks.shape[1], dtype=jnp.int32)[None, :]
    return jnp.einsum("fkc,tk->ftc", blocks, chosen.astype(blocks.dtype))


def forward_block(values, slots, live_count, columns, row_tiles, loop_count):
    channels = columns.shape[0]
    tile_len = values.shape[-1]
    col_tiles = columns.shape[1] // tile_len
    blocks = columns.reshape(channels, col_tiles, tile_len)

    def forward_add_group(group_idx, running):
        first_tile = group_idx * 8
        is_live = first_tile + jnp.arange(8, dtype=jnp.int32) < live_count
        picked = pick_blocks(blocks, slots % col_tiles)
        products = jnp.einsum("ftc,trc->tfr", picked, values, preferred_element_type=jnp.float32)
        target = (
            (slots // col_tiles)[:, None] == jnp.arange(row_tiles, dtype=jnp.int32)[None, :]
        ) & is_live[:, None]
        return running + jnp.einsum(
            "tfr,tk->fkr", products, target.astype(jnp.float32), precision=lax.Precision.HIGHEST
        )

    running = lax.fori_loop(
        0, loop_count, forward_add_group, jnp.zeros((channels, row_tiles, tile_len), jnp.float32)
    )
    return running.reshape(channels, row_tiles * tile_len)


def backward_block(values, slots, live_count, rows, col_tiles, loop_count):
    channels = rows.shape[0]
    tile_len = values.shape[-1]
    row_tiles = rows.shape[1] // tile_len
    blocks = rows.reshape(channels, row_tiles, tile_len)

    def backward_add_group(group_idx, running):
        first_tile = group_idx * 8
        is_live = first_tile + jnp.arange(8, dtype=jnp.int32) < live_count
        picked = pick_blocks(blocks, slots // col_tiles)
        products = jnp.einsum("ftr,trc->tfc", picked, values, preferred_element_type=jnp.float32)
        target = (
            (slots % col_tiles)[:, None] == jnp.arange(col_tiles, dtype=jnp.int32)[None, :]
        ) & is_live[:, None]
        return running + jnp.einsum(
            "tfc,tk->fkc", products, target.astype(jnp.float32), precision=lax.Precision.HIGHEST
        )

    running = lax.fori_loop(
        0, loop_count, backward_add_group, jnp.zeros((channels, col_tiles, tile_len), jnp.float32)
    )
    return running.reshape(channels, col_tiles * tile_len)


def per_device(input_feat, weight, tile_values, tile_slots, tile_count, grad_output):
    values = tile_values[0, 0]
    slots = tile_slots[0, 0]
    live_count = tile_count[0, 0]
    tile_len = values.shape[-1]
    row_tiles = grad_output.shape[1] // tile_len
    col_tiles = input_feat.shape[1] // tile_len
    loop_count = values.shape[0] // 8
    partial_agg = forward_block(
        values,
        slots,
        live_count,
        gather(input_feat, "row"),
        row_tiles,
        loop_count,
    )
    aggregate = gather(scatter_sum(partial_agg.astype(jnp.bfloat16), "col").astype(jnp.bfloat16), "col")
    out_width = weight.shape[1] // lax.axis_size("col")
    weight_cols = lax.dynamic_slice_in_dim(weight, lax.axis_index("col") * out_width, out_width, 1)
    pre_act = lax.dot_general(
        weight_cols, aggregate, (((0,), (0,)), ((), ())), preferred_element_type=jnp.float32
    )
    sigmoid = jax.nn.sigmoid(pre_act)
    output_feat = (pre_act * sigmoid).astype(jnp.bfloat16)
    grad_pre = (
        grad_output.astype(jnp.float32) * sigmoid * (1.0 + pre_act * (1.0 - sigmoid))
    ).astype(jnp.bfloat16)
    weight_part = lax.dot_general(
        aggregate, grad_pre, (((1,), (1,)), ((), ())), preferred_element_type=jnp.float32
    )
    grad_full = gather(grad_pre, "col")
    grad_agg = jnp.dot(weight, grad_full, preferred_element_type=jnp.float32).astype(jnp.bfloat16)
    input_part = backward_block(values, slots, live_count, grad_agg, col_tiles, loop_count)
    grad_input = scatter_sum(input_part.astype(jnp.bfloat16), "row")
    weight_share = scatter_sum(weight_part.astype(jnp.bfloat16), "row")
    node_total = grad_output.shape[1] * lax.axis_size("row")
    return (output_feat, weight_share * node_total ** (-0.5), grad_input)


def solution(mesh):
    in_specs = (
        P("row", "col"),
        P(),
        P("row", "col", None, None, None),
        P("row", "col", None),
        P("row", "col"),
        P("col", "row"),
    )
    out_specs = (P("col", "row"), P("row", "col"), P("row", "col"))
    R, C = mesh.shape["row"], mesh.shape["col"]

    def device(x, w, tv, slots, count, go):
        if R % 2 == 0 and go.shape[1] % (C * tv.shape[-1]) == 0 and x.shape[0] % 16 == 0:
            return fused_device(R, C, x, w, tv, slots, count, go)
        return per_device(x, w, tv, slots, count, go)

    return jax.shard_map(
        device, mesh=mesh, in_specs=in_specs, out_specs=out_specs, check_vma=False
    )
```
